512 devices in a mesh: seqa: 16 (over z_lo, core), seqb: 32 (over y, z_hi, x).
Axes of the slice: x: 4, y: 4, z: 16 (z_hi: 2, z_lo: 8; z = z_hi * 8 + z_lo), core: 2. Of those that a mesh axis runs over, the one named last changes fastest.
Arguments:
- sequence_input: bfloat16 [262144, 640], P(('seqa', 'seqb')), may hold values from -6 to 6
- w_prev: bfloat16 [3, 640, 1280], P(None, 'seqa'), may hold values from -0.15625 to 0.15625
- w_now: bfloat16 [3, 640, 1280], P(None, 'seqa'), may hold values from -0.15625 to 0.15625
- conv_bias: float32 [3, 1280], replicated, may hold values from -4 to 4
- w_mix: bfloat16 [3, 640, 640], P(None, None, 'seqa'), may hold values from -0.25 to 0.25
Outputs:
- seq_out: bfloat16 [262144, 640], P(('seqa', 'seqb'))
The draws below stay inside these ranges and needn't reach their ends.
All inputs are finite; a program needn't handle non-finite values.
Results may differ from the reference program's by a relative error of at most 0.0052.
Values may be sent and summed in bfloat16 or wider, within the bound.
No kernel may reach another device: no remote copies, remote signals or barrier semaphores. Data moves between devices by JAX's collectives and lax.ppermute only.
A program may use at most 64 MiB of HBM per device.

```python
import jax
import jax.numpy as jnp
from jax import lax

D = 640
LAYERS = 3
DILATION_FIRST1 = 128
DILATION_SECOND2 = 512
DILATION_THIRD3 = 2048
TOTAL = 262144


def shard_levels(key, extent, shards, low, largest):
    level, own = 1.0, jax.random.fold_in(key, 6)
    for axis_at, blocks in shards:
        draws = jnp.exp(jax.random.uniform(jax.random.fold_in(own, axis_at), (blocks,), jnp.float32, low / len(shards), largest / len(shards)))
        level = level * jnp.repeat(draws, extent[axis_at] // blocks).reshape([-1 if axis == axis_at else 1 for axis in range(len(extent))])
    return level


def gaussian(rng, shape, width, most, cuts=(), held_as=jnp.bfloat16):
    factor_of = shard_levels(rng, shape, cuts, -0.22, 0.18) if cuts else 1.0
    array = jax.random.normal(rng, shape, jnp.float32) * width * factor_of
    return jnp.minimum(jnp.maximum(array, -most), most).astype(held_as)


def setup_inputs(seed: int = 0) -> dict:
    arg_keys = jax.random.split(jax.random.key(seed), 6)
    sequence_input = gaussian(arg_keys[0], (TOTAL, D), 1.0, 6.0, ((0, 512),))
    w_prev = gaussian(arg_keys[1], (LAYERS, D, 2 * D), (2 * D) ** -0.5, 0.15625, ((1, 16),))
    w_now = gaussian(arg_keys[2], (LAYERS, D, 2 * D), (2 * D) ** -0.5, 0.15625, ((1, 16),))
    conv_bias = gaussian(arg_keys[3], (LAYERS, 2 * D), 1.0, 4.0, (), jnp.float32)
    w_mix = gaussian(arg_keys[4], (LAYERS, D, D), D ** -0.5, 0.25, ((2, 16),))
    return dict(sequence_input=sequence_input, w_prev=w_prev, w_now=w_now, conv_bias=conv_bias, w_mix=w_mix)


def norm_rows(values):
    scale = lax.rsqrt(lax.optimization_barrier(jnp.mean(values * values, axis=1, keepdims=True)) + 1e-06)
    return (values * scale).astype(jnp.bfloat16)

def reference(sequence_input, w_prev, w_now, conv_bias, w_mix):
    hidden_state = sequence_input.astype(jnp.float32)
    for layer_index, dilation_step in enumerate((DILATION_FIRST1, DILATION_SECOND2, DILATION_THIRD3)):
        normed = norm_rows(hidden_state)
        earlier = jnp.pad(normed, ((dilation_step, 0), (0, 0)))[:normed.shape[0]]
        pre = jnp.dot(earlier, w_prev[layer_index], preferred_element_type=jnp.float32)
        pre = pre + jnp.dot(normed, w_now[layer_index], preferred_element_type=jnp.float32)
        pre = pre + conv_bias[layer_index]
        hidden = (pre[:, :D] * jax.nn.sigmoid(pre[:, D:])).astype(jnp.bfloat16)
        hidden_state = hidden_state + jnp.dot(hidden, w_mix[layer_index], preferred_element_type=jnp.float32)
    return hidden_state.astype(jnp.bfloat16)
```

```python
import jax
import jax.numpy as jnp
from jax import lax
from jax.experimental import pallas as pl
from jax.experimental.pallas import tpu as pltpu
from jax.sharding import Mesh
from jax.sharding import PartitionSpec as P

D = 640
BLOCK = 512
TAIL = 128
TILE = 256
AXES = ("zl", "core", "y", "zh", "x")
SIZES = (8, 2, 4, 2, 4)
DEVICES = 512
Z_SLOTS = (-1, 0, 1, 2, 3, 4, -3, -2)


def index_of(z, core, y, x):
    z, y, x = z % 16, y % 4, x % 4
    return (((z % 8) * 2 + core) * 4 + y) * 8 + (z // 8) * 4 + x


def permuted(value, target):
    pairs = []
    for z in range(16):
        for core in range(2):
            for y in range(4):
                for x in range(4):
                    pairs.append((index_of(z, core, y, x), index_of(*target(z, core, y, x))))
    return lax.ppermute(value, AXES, pairs)


def shifted(value, target):
    pairs = [(b, target(b)) for b in range(DEVICES)]
    return lax.ppermute(value, AXES, [(a, b) for a, b in pairs if b < DEVICES])


def from_z(value, by):
    return permuted(value, lambda z, core, y, x: (z - by, core, y, x))


def from_first(value, by):
    return permuted(
        value, lambda z, core, y, x: (z, core, y, x - by) if core == 0 else (z, core, y - by, x)
    )


def from_second(value, by):
    return permuted(
        value, lambda z, core, y, x: (z, core, y - by, x) if core == 0 else (z, core, y, x - by)
    )


def from_sibling(value):
    return permuted(value, lambda z, core, y, x: (z, 1 - core, y, x))


def normed(values):
    scale = lax.rsqrt(jnp.mean(values * values, axis=1, keepdims=True) + 1e-06)
    return (values * scale).astype(jnp.bfloat16)


def kernel(
    where, s_ref, a_ref, r_ref, b_ref, ts_ref, tr_ref, perm_ref, bias_ref,
    g0, g1, g2, g3, h0, h1, h2, h3,
    out_ref, taps, mix, x0, u1, u2, x1, u3, sems,
):
    x, y, core = where[0], where[1], where[2]
    for half, arrays in enumerate(((g0, g1, g2, g3), (h0, h1, h2, h3))):
        x_first = (core + half) % 2 == 0
        for j in range(4):
            for i in range(4):
                px = (x + jnp.where(x_first, i, j)) % 4
                py = (y + jnp.where(x_first, j, i)) % 4
                rows = pl.multiple_of((px // 2) * D + half * 320, 320)
                columns = pl.multiple_of((px % 2) * D, D)
                source = arrays[j].at[i]

                @pl.when(py < 3)
                def _():
                    pltpu.make_async_copy(
                        source, taps.at[py, pl.ds(rows, 320), pl.ds(columns, D)], sems.at[py]
                    ).start()

                @pl.when((py == 3) & (px < 3))
                def _():
                    pltpu.make_async_copy(
                        source, mix.at[px, pl.ds(half * 320, 320)], sems.at[3]
                    ).start()

    def bring(ref, slot, tail_slot, start, count):
        exact = jnp.dot(ref[start : start + count], perm_ref[...], preferred_element_type=jnp.float32)
        x0[slot, start : start + count] = exact.astype(jnp.bfloat16)
        unit = normed(exact)
        u1[slot, TAIL + start : TAIL + start + count] = unit
        if tail_slot is not None and start + count == BLOCK:
            u1[tail_slot, :TAIL] = unit[count - TAIL :]

    def bring_tail(ref, slot):
        exact = jnp.dot(ref[...], perm_ref[...], preferred_element_type=jnp.float32)
        u1[slot, :TAIL] = normed(exact)

    a_slot = jnp.where(x == 0, 0, 2)
    t_slot = jnp.where(x < 2, 0, 2)
    for start in range(0, BLOCK, TILE):
        bring(s_ref, 3, None, start, TILE)
        bring(r_ref, 1, None, start, TILE)
        bring(a_ref, a_slot, a_slot + 1, start, TILE)
        bring(b_ref, 2 - a_slot, 3 - a_slot, start, TILE)
    bring_tail(ts_ref, t_slot)
    bring_tail(tr_ref, 2 - t_slot)

    def layer(prev, now, held, index):
        both = jnp.concatenate([prev, now], axis=1)
        pre = jnp.dot(both, taps[index], preferred_element_type=jnp.float32)
        pre = pre + bias_ref[index : index + 1, :]
        hidden = (pre[:, :D] * jax.nn.sigmoid(pre[:, D:])).astype(jnp.bfloat16)
        return held + lax.dot_general(
            hidden, mix[index], (((1,), (1,)), ((), ())), preferred_element_type=jnp.float32
        )

    pltpu.make_async_copy(mix, mix, sems.at[3]).wait()
    pltpu.make_async_copy(taps.at[0], taps.at[0], sems.at[0]).wait()

    @pl.loop(0, 8)
    def _(step):
        slot = step // 2
        start = pl.multiple_of((step % 2) * TILE, TILE)
        rows = pl.ds(start, TILE)
        now = u1[slot, pl.ds(pl.multiple_of(start + TAIL, TAIL), TILE)]
        after = layer(u1[slot, rows], now, x0[slot, rows].astype(jnp.float32), 0)
        unit = normed(after)
        u2[slot, rows] = jnp.where(where[3 + slot] != 0, unit, jnp.zeros_like(unit))
        x1[slot, rows] = after

    pltpu.make_async_copy(taps.at[1], taps.at[1], sems.at[1]).wait()

    @pl.loop(0, 4)
    def _(step):
        slot = (step // 2) * 2 + 1
        rows = pl.ds(pl.multiple_of((step % 2) * TILE, TILE), TILE)
        after = layer(u2[slot - 1, rows], u2[slot, rows], x1[slot, rows], 1)
        unit = normed(after)
        u3[step // 2, rows] = jnp.where(where[3 + slot] != 0, unit, jnp.zeros_like(unit))
        x1[slot, rows] = after

    pltpu.make_async_copy(taps.at[2], taps.at[2], sems.at[2]).wait()

    @pl.loop(0, 2)
    def _(step):
        rows = pl.ds(pl.multiple_of(step * TILE, TILE), TILE)
        after = layer(u3[0, rows], u3[1, rows], x1[3, rows], 2).astype(jnp.bfloat16)
        out_ref[rows, :] = lax.dot_general(
            after, perm_ref[...], (((1,), (1,)), ((), ())), preferred_element_type=jnp.float32
        ).astype(jnp.bfloat16)


def block_output(where, rows_in, perm, bias, weights):
    vmem = pl.BlockSpec(memory_space=pltpu.VMEM)
    hbm = pl.BlockSpec(memory_space=pl.ANY)
    return pl.pallas_call(
        kernel,
        out_shape=jax.ShapeDtypeStruct((BLOCK, D), jnp.bfloat16),
        in_specs=[pl.BlockSpec(memory_space=pltpu.SMEM)] + [vmem] * 8 + [hbm] * 8,
        out_specs=vmem,
        scratch_shapes=[
            pltpu.VMEM((3, 2 * D, 2 * D), jnp.bfloat16),
            pltpu.VMEM((3, D, D), jnp.bfloat16),
            pltpu.VMEM((4, BLOCK, D), jnp.bfloat16),
            pltpu.VMEM((4, TAIL + BLOCK, D), jnp.bfloat16),
            pltpu.VMEM((4, BLOCK, D), jnp.bfloat16),
            pltpu.VMEM((4, BLOCK, D), jnp.float32),
            pltpu.VMEM((2, BLOCK, D), jnp.bfloat16),
            pltpu.SemaphoreType.DMA((4,)),
        ],
        compiler_params=pltpu.CompilerParams(vmem_limit_bytes=56 * 1024 * 1024),
        cost_estimate=pl.CostEstimate(flops=15_000_000_000, bytes_accessed=16_000_000, transcendentals=3_000_000),
    )(where, *rows_in, perm, bias, *weights)


def local(sequence_input, w_prev, w_now, conv_bias, w_mix):
    zl, core, y, zh, x = (lax.axis_index(a) for a in AXES)
    block = (((zl * 2 + core) * 4 + y) * 2 + zh) * 4 + x

    at = jnp.minimum(y, 2)
    tap_prev = lax.dynamic_slice(w_prev, (at, 0, (x % 2) * D), (1, 40, D))[0]
    tap_now = lax.dynamic_slice(w_now, (at, 0, (x % 2) * D), (1, 40, D))[0]
    mixing = lax.dynamic_slice(w_mix, (jnp.minimum(x, 2), 0, 0), (1, D, 40))[0].T
    piece = jnp.where(y == 3, mixing, jnp.where(x < 2, tap_prev, tap_now))

    above, below = from_z(piece, 1), from_z(piece, -1)
    three = jnp.concatenate([below, piece, above])
    far_above, far_below = from_z(three, 3), from_z(three[40:], -3)
    whole = jnp.concatenate([three, far_above, far_below])

    own = sequence_input
    far = shifted(own, lambda b: b + 4)
    beside = shifted(own, lambda b: b + 1 if b % 4 < 3 else b + 5)
    own_tail = shifted(own[BLOCK - TAIL :], lambda b: b + 2 if b % 4 < 2 else b + 6)
    far_beside = permuted(far, lambda z, c, yy, xx: (z, c, yy, xx + 1))
    far_tail = permuted(far[BLOCK - TAIL :], lambda z, c, yy, xx: (z, c, yy, xx + 2))

    line = jnp.stack([whole] + [from_first(whole, by) for by in (1, 2, 3)])
    mine = [line] + [from_second(line, by) for by in (1, 2, 3)]
    theirs = [from_sibling(v) for v in mine]

    k = jnp.arange(D)
    slot = (k % 320) // 40
    shard = (zl + jnp.asarray(Z_SLOTS, jnp.int32)[slot]) % 8
    channel = (shard * 2 + jnp.where(k < 320, core, 1 - core)) * 40 + k % 40
    perm = (k[:, None] == channel[None, :]).astype(jnp.bfloat16)

    where = jnp.stack(
        [x, y, core, block >= 5, block >= 4, block >= 1, block >= 0, block]
    ).astype(jnp.int32)
    rows_in = (own, beside, far, far_beside, own_tail, far_tail)
    return block_output(where, rows_in, perm, conv_bias, mine + theirs)


def solution(mesh):
    finer = Mesh(mesh.devices.reshape(SIZES), AXES)
    seqa, seqb = AXES[:2], AXES[2:]
    in_specs = (P(AXES, None), P(None, seqa, None), P(None, seqa, None), P(), P(None, None, seqa))
    return jax.shard_map(
        local, mesh=finer, in_specs=in_specs, out_specs=P(AXES, None), check_vma=False
    )
```

```python
import jax
import jax.numpy as jnp
from jax import lax
from jax.experimental import pallas as pl
from jax.experimental.pallas import tpu as pltpu
from jax.sharding import Mesh
from jax.sharding import PartitionSpec as P

D = 640
LAYERS = 3
BLOCK = 512
TAIL = 128
AXES = ("zl", "core", "y", "zh", "x")
SIZES = (8, 2, 4, 2, 4)
DEVICES = 512
Z_SLOTS = (-1, 0, 1, 2, 3, 4, -3, -2)


def index_of(z, core, y, x):
    z, y, x = z % 16, y % 4, x % 4
    return (((z % 8) * 2 + core) * 4 + y) * 8 + (z // 8) * 4 + x


def permuted(value, target):
    pairs = []
    for z in range(16):
        for core in range(2):
            for y in range(4):
                for x in range(4):
                    pairs.append((index_of(z, core, y, x), index_of(*target(z, core, y, x))))
    return lax.ppermute(value, AXES, pairs)


def shifted(value, target):
    pairs = [(b, target(b)) for b in range(DEVICES)]
    return lax.ppermute(value, AXES, [(a, b) for a, b in pairs if b < DEVICES])


def from_z(value, by):
    return permuted(value, lambda z, core, y, x: (z - by, core, y, x))


def normed(values):
    scale = lax.rsqrt(jnp.mean(values * values, axis=1, keepdims=True) + 1e-06)
    return (values * scale).astype(jnp.bfloat16)


def kernel(
    where, s_ref, a_ref, r_ref, b_ref, ts_ref, tr_ref, perm_ref, bias_ref,
    gathered, out_ref, taps, mix, x0, u1, u2, x1, u3, sems,
):
    x = where[0]

    def fetch(px, py, target, sem):
        for half in range(2):
            pltpu.make_async_copy(gathered.at[half * 16 + py * 4 + px], target(half * 320), sem).start()

    def fetch_mix(layer):
        fetch(layer, 3, lambda row: mix.at[layer, pl.ds(row, 320)], sems.at[3 + layer])

    def fetch_taps(layer):
        for px in range(4):
            rows, columns = (px // 2) * D, pl.ds((px % 2) * D, D)
            fetch(px, layer, lambda row: taps.at[layer, pl.ds(rows + row, 320), columns], sems.at[layer])

    for index in range(LAYERS):
        fetch_taps(index)
        fetch_mix(index)

    def ready(layer):
        pltpu.make_async_copy(taps.at[layer], taps.at[layer], sems.at[layer]).wait()
        pltpu.make_async_copy(mix.at[layer], mix.at[layer], sems.at[3 + layer]).wait()

    def bring(ref, slot, tail_slot):
        exact = jnp.dot(ref[...], perm_ref[...], preferred_element_type=jnp.float32)
        x0[slot] = exact.astype(jnp.bfloat16)
        unit = normed(exact)
        u1[slot, TAIL:] = unit
        if tail_slot is not None:
            u1[tail_slot, :TAIL] = unit[BLOCK - TAIL :]

    def bring_tail(ref, slot):
        exact = jnp.dot(ref[...], perm_ref[...], preferred_element_type=jnp.float32)
        u1[slot, :TAIL] = normed(exact)

    a_slot = jnp.where(x == 0, 0, 2)
    t_slot = jnp.where(x < 2, 0, 2)
    bring(s_ref, 3, None)
    bring(r_ref, 1, None)
    bring(a_ref, a_slot, a_slot + 1)
    bring(b_ref, 2 - a_slot, 3 - a_slot)
    bring_tail(ts_ref, t_slot)
    bring_tail(tr_ref, 2 - t_slot)

    def layer(prev, now, held, index):
        both = jnp.concatenate([prev, now], axis=1)
        pre = jnp.dot(both, taps[index], preferred_element_type=jnp.float32)
        pre = pre + bias_ref[index : index + 1, :]
        hidden = (pre[:, :D] * jax.nn.sigmoid(pre[:, D:])).astype(jnp.bfloat16)
        return held + lax.dot_general(
            hidden, mix[index], (((1,), (1,)), ((), ())), preferred_element_type=jnp.float32
        )

    ready(0)

    def keep(slot, unit):
        return jnp.where(where[1 + slot] != 0, unit, jnp.zeros_like(unit))

    def two(ref, first, second, rows):
        return jnp.concatenate([ref[first, rows], ref[second, rows]], axis=0)

    def first_layer(pair):
        low, high = 2 * pair, 2 * pair + 1
        prev = two(u1, low, high, pl.ds(0, BLOCK))
        now = two(u1, low, high, pl.ds(TAIL, BLOCK))
        after = layer(prev, now, two(x0, low, high, pl.ds(0, BLOCK)).astype(jnp.float32), 0)
        unit = normed(after)
        u2[low] = keep(low, unit[:BLOCK])
        u2[high] = keep(high, unit[BLOCK:])
        x1[pair] = after[BLOCK:]

    pl.loop(0, 2)(first_layer)

    ready(1)
    after = layer(two(u2, 0, 2, slice(None)), two(u2, 1, 3, slice(None)), jnp.concatenate([x1[0], x1[1]], axis=0), 1)
    unit = normed(after)
    u3[0] = keep(1, unit[:BLOCK])
    u3[1] = unit[BLOCK:]
    x1[1] = after[BLOCK:]

    ready(2)
    after = layer(u3[0], u3[1], x1[1], 2).astype(jnp.bfloat16)
    out_ref[...] = lax.dot_general(
        after, perm_ref[...], (((1,), (1,)), ((), ())), preferred_element_type=jnp.float32
    ).astype(jnp.bfloat16)


def block_output(where, rows_in, perm, bias, weights):
    vmem = pl.BlockSpec(memory_space=pltpu.VMEM)
    hbm = pl.BlockSpec(memory_space=pl.ANY)
    return pl.pallas_call(
        kernel,
        out_shape=jax.ShapeDtypeStruct((BLOCK, D), jnp.bfloat16),
        in_specs=[pl.BlockSpec(memory_space=pltpu.SMEM)] + [vmem] * 8 + [hbm],
        out_specs=vmem,
        scratch_shapes=[
            pltpu.VMEM((3, 2 * D, 2 * D), jnp.bfloat16),
            pltpu.VMEM((3, D, D), jnp.bfloat16),
            pltpu.VMEM((4, BLOCK, D), jnp.bfloat16),
            pltpu.VMEM((4, TAIL + BLOCK, D), jnp.bfloat16),
            pltpu.VMEM((4, BLOCK, D), jnp.bfloat16),
            pltpu.VMEM((2, BLOCK, D), jnp.float32),
            pltpu.VMEM((2, BLOCK, D), jnp.bfloat16),
            pltpu.SemaphoreType.DMA((6,)),
        ],
        compiler_params=pltpu.CompilerParams(vmem_limit_bytes=56 * 1024 * 1024),
        cost_estimate=pl.CostEstimate(flops=15_000_000_000, bytes_accessed=16_000_000, transcendentals=3_000_000),
    )(where, *rows_in, perm, bias, weights)


def local(sequence_input, w_prev, w_now, conv_bias, w_mix):
    zl, core, y, zh, x = (lax.axis_index(a) for a in AXES)
    block = (((zl * 2 + core) * 4 + y) * 2 + zh) * 4 + x

    at = jnp.minimum(y, 2)
    tap_prev = lax.dynamic_slice(w_prev, (at, 0, (x % 2) * D), (1, 40, D))[0]
    tap_now = lax.dynamic_slice(w_now, (at, 0, (x % 2) * D), (1, 40, D))[0]
    mixing = lax.dynamic_slice(w_mix, (jnp.minimum(x, 2), 0, 0), (1, D, 40))[0].T
    piece = jnp.where(y == 3, mixing, jnp.where(x < 2, tap_prev, tap_now))

    own = sequence_input
    stepped = lax.ppermute(
        own, AXES, [(b, b + 8) for b in range(DEVICES) if b % 8 >= 4 and b + 8 < DEVICES]
    )
    above, below = from_z(piece, 1), from_z(piece, -1)
    three = jnp.concatenate([below, piece, above])
    far_above, far_below = from_z(three, 3), from_z(three[40:], -3)
    near = jnp.concatenate([three, far_above, far_below])

    k = jnp.arange(D)
    shard = (zl + jnp.asarray(Z_SLOTS, jnp.int32)[(k % 320) // 40]) % 8
    channel = (shard * 2 + k // 320) * 40 + k % 40
    perm = (k[:, None] == channel[None, :]).astype(jnp.bfloat16)
    where = jnp.stack([x, block >= 5, block >= 4, block >= 1, block >= 0]).astype(jnp.int32)
    near, own, stepped, perm, where = lax.optimization_barrier((near, own, stepped, perm, where))

    weights = lax.all_gather(near, ("core", "y", "x"))
    far = permuted(
        jnp.where(zh == 1, stepped, own), lambda z, c, yy, xx: (z + 8, c, yy, xx)
    )
    beside = shifted(own, lambda b: b + 1 if b % 4 < 3 else b + 5)
    own_tail = shifted(own[BLOCK - TAIL :], lambda b: b + 2 if b % 4 < 2 else b + 6)
    far, beside, own_tail = lax.optimization_barrier((far, beside, own_tail))
    far_beside = permuted(far, lambda z, c, yy, xx: (z, c, yy, xx + 1))
    far_tail = permuted(far[BLOCK - TAIL :], lambda z, c, yy, xx: (z, c, yy, xx + 2))

    rows_in = (own, beside, far, far_beside, own_tail, far_tail)
    return block_output(where, rows_in, perm, conv_bias, weights)


def solution(mesh):
    finer = Mesh(mesh.devices.reshape(SIZES), AXES)
    seqa, seqb = AXES[:2], AXES[2:]
    in_specs = (P(AXES, None), P(None, seqa, None), P(None, seqa, None), P(), P(None, None, seqa))
    return jax.shard_map(
        local, mesh=finer, in_specs=in_specs, out_specs=P(AXES, None), check_vma=False
    )
```

```python
import jax
import jax.numpy as jnp
from jax import lax
from jax.experimental import pallas as pl
from jax.experimental.pallas import tpu as pltpu
from jax.sharding import Mesh
from jax.sharding import PartitionSpec as P

D = 640
LAYERS = 3
BLOCK = 512
TAIL = 128
AXES = ("zl", "core", "y", "zh", "x")
SIZES = (8, 2, 4, 2, 4)
DEVICES = 512
Z_SLOTS = (-1, 0, 1, 2, 3, 4, -3, -2)


def index_of(z, core, y, x):
    z, y, x = z % 16, y % 4, x % 4
    return (((z % 8) * 2 + core) * 4 + y) * 8 + (z // 8) * 4 + x


def permuted(value, target):
    pairs = []
    for z in range(16):
        for core in range(2):
            for y in range(4):
                for x in range(4):
                    pairs.append((index_of(z, core, y, x), index_of(*target(z, core, y, x))))
    return lax.ppermute(value, AXES, pairs)


def shifted(value, target):
    pairs = [(b, target(b)) for b in range(DEVICES)]
    return lax.ppermute(value, AXES, [(a, b) for a, b in pairs if b < DEVICES])


def from_z(value, by):
    return permuted(value, lambda z, core, y, x: (z - by, core, y, x))


def normed(values):
    scale = lax.rsqrt(jnp.mean(values * values, axis=1, keepdims=True) + 1e-06)
    return (values * scale).astype(jnp.bfloat16)


def kernel(
    where, s_ref, a_ref, r_ref, b_ref, ts_ref, tr_ref, perm_ref, bias_ref,
    gathered, out_ref, taps, mix, x0, u1, u2, x1, u3, sems,
):
    x = where[0]

    def fetch(px, py, target, sem):
        for half in range(2):
            pltpu.make_async_copy(gathered.at[half * 16 + py * 4 + px], target(half * 320), sem).start()

    def fetch_mix(layer):
        fetch(layer, 3, lambda row: mix.at[layer, pl.ds(row, 320)], sems.at[3 + layer])

    def fetch_taps(layer):
        for px in range(4):
            rows, columns = (px // 2) * D, pl.ds((px % 2) * D, D)
            fetch(px, layer, lambda row: taps.at[layer, pl.ds(rows + row, 320), columns], sems.at[layer])

    for index in range(LAYERS):
        fetch_taps(index)
        fetch_mix(index)

    def ready(layer):
        pltpu.make_async_copy(taps.at[layer], taps.at[layer], sems.at[layer]).wait()
        pltpu.make_async_copy(mix.at[layer], mix.at[layer], sems.at[3 + layer]).wait()

    def bring(ref, slot, tail_slot):
        x0[slot] = ref[...]
        unit = normed(ref[...].astype(jnp.float32))
        u1[slot, TAIL:] = unit
        if tail_slot is not None:
            u1[tail_slot, :TAIL] = unit[BLOCK - TAIL :]

    def bring_tail(ref, slot):
        u1[slot, :TAIL] = normed(ref[...].astype(jnp.float32))

    a_slot = jnp.where(x == 0, 0, 2)
    t_slot = jnp.where(x < 2, 0, 2)
    bring(s_ref, 3, None)
    bring(r_ref, 1, None)
    bring(a_ref, a_slot, a_slot + 1)
    bring(b_ref, 2 - a_slot, 3 - a_slot)
    bring_tail(ts_ref, t_slot)
    bring_tail(tr_ref, 2 - t_slot)

    def layer(prev, now, held, index):
        both = jnp.concatenate([prev, now], axis=1)
        pre = jnp.dot(both, taps[index], preferred_element_type=jnp.float32)
        pre = pre + bias_ref[index : index + 1, :]
        hidden = (pre[:, :D] * jax.nn.sigmoid(pre[:, D:])).astype(jnp.bfloat16)
        return held + lax.dot_general(
            hidden, mix[index], (((1,), (1,)), ((), ())), preferred_element_type=jnp.float32
        )

    ready(0)

    def keep(slot, unit):
        return jnp.where(where[1 + slot] != 0, unit, jnp.zeros_like(unit))

    def two(ref, first, second, rows):
        return jnp.concatenate([ref[first, rows], ref[second, rows]], axis=0)

    def first_layer(pair):
        low, high = 2 * pair, 2 * pair + 1
        prev = two(u1, low, high, pl.ds(0, BLOCK))
        now = two(u1, low, high, pl.ds(TAIL, BLOCK))
        after = layer(prev, now, two(x0, low, high, pl.ds(0, BLOCK)).astype(jnp.float32), 0)
        unit = normed(after)
        u2[low] = keep(low, unit[:BLOCK])
        u2[high] = keep(high, unit[BLOCK:])
        x1[pair] = after[BLOCK:]

    pl.loop(0, 2)(first_layer)

    ready(1)
    after = layer(two(u2, 0, 2, slice(None)), two(u2, 1, 3, slice(None)), jnp.concatenate([x1[0], x1[1]], axis=0), 1)
    unit = normed(after)
    u3[0] = keep(1, unit[:BLOCK])
    u3[1] = unit[BLOCK:]
    x1[1] = after[BLOCK:]

    ready(2)
    after = layer(u3[0], u3[1], x1[1], 2).astype(jnp.bfloat16)
    out_ref[...] = lax.dot_general(
        after, perm_ref[...], (((1,), (1,)), ((), ())), preferred_element_type=jnp.float32
    ).astype(jnp.bfloat16)


def block_output(where, rows_in, perm, bias, weights):
    vmem = pl.BlockSpec(memory_space=pltpu.VMEM)
    hbm = pl.BlockSpec(memory_space=pl.ANY)
    return pl.pallas_call(
        kernel,
        out_shape=jax.ShapeDtypeStruct((BLOCK, D), jnp.bfloat16),
        in_specs=[pl.BlockSpec(memory_space=pltpu.SMEM)] + [vmem] * 8 + [hbm],
        out_specs=vmem,
        scratch_shapes=[
            pltpu.VMEM((3, 2 * D, 2 * D), jnp.bfloat16),
            pltpu.VMEM((3, D, D), jnp.bfloat16),
            pltpu.VMEM((4, BLOCK, D), jnp.bfloat16),
            pltpu.VMEM((4, TAIL + BLOCK, D), jnp.bfloat16),
            pltpu.VMEM((4, BLOCK, D), jnp.bfloat16),
            pltpu.VMEM((2, BLOCK, D), jnp.float32),
            pltpu.VMEM((2, BLOCK, D), jnp.bfloat16),
            pltpu.SemaphoreType.DMA((6,)),
        ],
        compiler_params=pltpu.CompilerParams(vmem_limit_bytes=56 * 1024 * 1024),
        cost_estimate=pl.CostEstimate(flops=15_000_000_000, bytes_accessed=16_000_000, transcendentals=3_000_000),
    )(where, *rows_in, perm, bias, weights)


def local(sequence_input, w_prev, w_now, conv_bias, w_mix):
    zl, core, y, zh, x = (lax.axis_index(a) for a in AXES)
    block = (((zl * 2 + core) * 4 + y) * 2 + zh) * 4 + x

    at = jnp.minimum(y, 2)
    tap_prev = lax.dynamic_slice(w_prev, (at, 0, (x % 2) * D), (1, 40, D))[0]
    tap_now = lax.dynamic_slice(w_now, (at, 0, (x % 2) * D), (1, 40, D))[0]
    mixing = lax.dynamic_slice(w_mix, (jnp.minimum(x, 2), 0, 0), (1, D, 40))[0].T
    piece = jnp.where(y == 3, mixing, jnp.where(x < 2, tap_prev, tap_now))

    own = sequence_input
    stepped = lax.ppermute(
        own, AXES, [(b, b + 8) for b in range(DEVICES) if b % 8 >= 4 and b + 8 < DEVICES]
    )
    above, below = from_z(piece, 1), from_z(piece, -1)
    three = jnp.concatenate([below, piece, above])
    far_above, far_below = from_z(three, 3), from_z(three[40:], -3)
    near = jnp.concatenate([three, far_above, far_below])

    k = jnp.arange(D)
    shard = (zl + jnp.asarray(Z_SLOTS, jnp.int32)[(k % 320) // 40]) % 8
    channel = (shard * 2 + k // 320) * 40 + k % 40
    perm = (k[:, None] == channel[None, :]).astype(jnp.bfloat16)
    where = jnp.stack([x, block >= 5, block >= 4, block >= 1, block >= 0]).astype(jnp.int32)
    near, own, stepped = lax.optimization_barrier((near, own, stepped))

    weights = lax.all_gather(near, ("core", "y", "x"))
    far = permuted(
        jnp.where(zh == 1, stepped, own), lambda z, c, yy, xx: (z + 8, c, yy, xx)
    )
    beside = shifted(own, lambda b: b + 1 if b % 4 < 3 else b + 5)
    own_tail = shifted(own[BLOCK - TAIL :], lambda b: b + 2 if b % 4 < 2 else b + 6)
    far, beside, own_tail, perm = lax.optimization_barrier((far, beside, own_tail, perm))

    def reordered(rows):
        return jnp.dot(rows, perm, preferred_element_type=jnp.float32).astype(jnp.bfloat16)

    far = reordered(far)
    far_beside = permuted(far, lambda z, c, yy, xx: (z, c, yy, xx + 1))
    far_tail = permuted(far[BLOCK - TAIL :], lambda z, c, yy, xx: (z, c, yy, xx + 2))

    own, beside, own_tail = reordered(own), reordered(beside), reordered(own_tail)
    rows_in = (own, beside, far, far_beside, own_tail, far_tail)
    return block_output(where, rows_in, perm, conv_bias, weights)


def solution(mesh):
    finer = Mesh(mesh.devices.reshape(SIZES), AXES)
    seqa, seqb = AXES[:2], AXES[2:]
    in_specs = (P(AXES, None), P(None, seqa, None), P(None, seqa, None), P(), P(None, None, seqa))
    return jax.shard_map(
        local, mesh=finer, in_specs=in_specs, out_specs=P(AXES, None), check_vma=False
    )
```

```python
import jax
import jax.numpy as jnp
from jax import lax
from jax.experimental import pallas as pl
from jax.experimental.pallas import tpu as pltpu
from jax.sharding import Mesh
from jax.sharding import PartitionSpec as P

D = 640
LAYERS = 3
BLOCK = 512
TAIL = 128
AXES = ("zl", "core", "y", "zh", "x")
SIZES = (8, 2, 4, 2, 4)
DEVICES = 512
Z_SLOTS = (-1, 0, 1, 2, 3, 4, -3, -2)


def index_of(z, core, y, x):
    z, y, x = z % 16, y % 4, x % 4
    return (((z % 8) * 2 + core) * 4 + y) * 8 + (z // 8) * 4 + x


def permuted(value, target):
    pairs = []
    for z in range(16):
        for core in range(2):
            for y in range(4):
                for x in range(4):
                    pairs.append((index_of(z, core, y, x), index_of(*target(z, core, y, x))))
    return lax.ppermute(value, AXES, pairs)


def shifted(value, target):
    pairs = [(b, target(b)) for b in range(DEVICES)]
    return lax.ppermute(value, AXES, [(a, b) for a, b in pairs if b < DEVICES])


def from_z(value, by):
    return permuted(value, lambda z, core, y, x: (z - by, core, y, x))


def normed(values):
    scale = lax.rsqrt(jnp.mean(values * values, axis=1, keepdims=True) + 1e-06)
    return (values * scale).astype(jnp.bfloat16)


def kernel(
    where, s_ref, a_ref, r_ref, b_ref, ts_ref, tr_ref, perm_ref, bias_ref,
    gathered, out_ref, taps, mix, x0, u1, u2, x1, u3, sems,
):
    x = where[0]

    def fetch(px, py, target, sem):
        for half in range(2):
            pltpu.make_async_copy(gathered.at[half * 16 + py * 4 + px], target(half * 320), sem).start()

    def fetch_mix(layer):
        fetch(layer, 3, lambda row: mix.at[layer, pl.ds(row, 320)], sems.at[3 + layer])

    def fetch_taps(layer):
        for px in range(4):
            rows, columns = (px // 2) * D, pl.ds((px % 2) * D, D)
            fetch(px, layer, lambda row: taps.at[layer, pl.ds(rows + row, 320), columns], sems.at[layer])

    for index in range(LAYERS):
        fetch_taps(index)
        fetch_mix(index)

    def ready(layer):
        pltpu.make_async_copy(taps.at[layer], taps.at[layer], sems.at[layer]).wait()
        pltpu.make_async_copy(mix.at[layer], mix.at[layer], sems.at[3 + layer]).wait()

    def bring(ref, slot, tail_slot):
        x0[slot] = ref[...]
        unit = normed(ref[...].astype(jnp.float32))
        u1[slot, TAIL:] = unit
        if tail_slot is not None:
            u1[tail_slot, :TAIL] = unit[BLOCK - TAIL :]

    def bring_tail(ref, slot):
        u1[slot, :TAIL] = normed(ref[...].astype(jnp.float32))

    a_slot = jnp.where(x == 0, 0, 2)
    t_slot = jnp.where(x < 2, 0, 2)
    bring(s_ref, 3, None)
    bring(r_ref, 1, None)
    bring(a_ref, a_slot, a_slot + 1)
    bring(b_ref, 2 - a_slot, 3 - a_slot)
    bring_tail(ts_ref, t_slot)
    bring_tail(tr_ref, 2 - t_slot)

    def layer(prev, now, held, index):
        both = jnp.concatenate([prev, now], axis=1)
        pre = jnp.dot(both, taps[index], preferred_element_type=jnp.float32)
        pre = pre + bias_ref[index : index + 1, :]
        hidden = (pre[:, :D] * jax.nn.sigmoid(pre[:, D:])).astype(jnp.bfloat16)
        return held + lax.dot_general(
            hidden, mix[index], (((1,), (1,)), ((), ())), preferred_element_type=jnp.float32
        )

    ready(0)

    def keep(slot, unit):
        return jnp.where(where[1 + slot] != 0, unit, jnp.zeros_like(unit))

    def two(ref, first, second, rows):
        return jnp.concatenate([ref[first, rows], ref[second, rows]], axis=0)

    def first_layer(pair):
        low, high = 2 * pair, 2 * pair + 1
        prev = two(u1, low, high, pl.ds(0, BLOCK))
        now = two(u1, low, high, pl.ds(TAIL, BLOCK))
        after = layer(prev, now, two(x0, low, high, pl.ds(0, BLOCK)).astype(jnp.float32), 0)
        unit = normed(after)
        u2[low] = keep(low, unit[:BLOCK])
        u2[high] = keep(high, unit[BLOCK:])
        x1[pair] = after[BLOCK:]

    pl.loop(0, 2)(first_layer)

    ready(1)
    after = layer(two(u2, 0, 2, slice(None)), two(u2, 1, 3, slice(None)), jnp.concatenate([x1[0], x1[1]], axis=0), 1)
    unit = normed(after)
    u3[0] = keep(1, unit[:BLOCK])
    u3[1] = unit[BLOCK:]
    x1[1] = after[BLOCK:]

    ready(2)
    after = layer(u3[0], u3[1], x1[1], 2).astype(jnp.bfloat16)
    out_ref[...] = lax.dot_general(
        after, perm_ref[...], (((1,), (1,)), ((), ())), preferred_element_type=jnp.float32
    ).astype(jnp.bfloat16)


def block_output(where, rows_in, perm, bias, weights):
    vmem = pl.BlockSpec(memory_space=pltpu.VMEM)
    hbm = pl.BlockSpec(memory_space=pl.ANY)
    return pl.pallas_call(
        kernel,
        out_shape=jax.ShapeDtypeStruct((BLOCK, D), jnp.bfloat16),
        in_specs=[pl.BlockSpec(memory_space=pltpu.SMEM)] + [vmem] * 8 + [hbm],
        out_specs=vmem,
        scratch_shapes=[
            pltpu.VMEM((3, 2 * D, 2 * D), jnp.bfloat16),
            pltpu.VMEM((3, D, D), jnp.bfloat16),
            pltpu.VMEM((4, BLOCK, D), jnp.bfloat16),
            pltpu.VMEM((4, TAIL + BLOCK, D), jnp.bfloat16),
            pltpu.VMEM((4, BLOCK, D), jnp.bfloat16),
            pltpu.VMEM((2, BLOCK, D), jnp.float32),
            pltpu.VMEM((2, BLOCK, D), jnp.bfloat16),
            pltpu.SemaphoreType.DMA((6,)),
        ],
        compiler_params=pltpu.CompilerParams(vmem_limit_bytes=56 * 1024 * 1024),
        cost_estimate=pl.CostEstimate(flops=15_000_000_000, bytes_accessed=16_000_000, transcendentals=3_000_000),
    )(where, *rows_in, perm, bias, weights)


def local(sequence_input, w_prev, w_now, conv_bias, w_mix):
    zl, core, y, zh, x = (lax.axis_index(a) for a in AXES)
    block = (((zl * 2 + core) * 4 + y) * 2 + zh) * 4 + x

    at = jnp.minimum(y, 2)
    tap_prev = lax.dynamic_slice(w_prev, (at, 0, (x % 2) * D), (1, 40, D))[0]
    tap_now = lax.dynamic_slice(w_now, (at, 0, (x % 2) * D), (1, 40, D))[0]
    mixing = lax.dynamic_slice(w_mix, (jnp.minimum(x, 2), 0, 0), (1, D, 40))[0].T
    piece = jnp.where(y == 3, mixing, jnp.where(x < 2, tap_prev, tap_now))

    own = sequence_input
    stepped = lax.ppermute(
        own, AXES, [(b, b + 8) for b in range(DEVICES) if b % 8 >= 4 and b + 8 < DEVICES]
    )
    above, below = from_z(piece, 1), from_z(piece, -1)
    three = jnp.concatenate([below, piece, above])
    far_above, far_below = from_z(three, 3), from_z(three[40:], -3)
    near = jnp.concatenate([three, far_above, far_below])

    k = jnp.arange(D)
    shard = (zl + jnp.asarray(Z_SLOTS, jnp.int32)[(k % 320) // 40]) % 8
    channel = (shard * 2 + k // 320) * 40 + k % 40
    perm = (k[:, None] == channel[None, :]).astype(jnp.bfloat16)
    where = jnp.stack([x, block >= 5, block >= 4, block >= 1, block >= 0]).astype(jnp.int32)
    beside = shifted(own, lambda b: b + 1 if b % 4 < 3 else b + 5)
    near, own, stepped, beside = lax.optimization_barrier((near, own, stepped, beside))

    weights = lax.all_gather(near, ("core", "y", "x"))
    far = permuted(
        jnp.where(zh == 1, stepped, own), lambda z, c, yy, xx: (z + 8, c, yy, xx)
    )
    own_tail = shifted(own[BLOCK - TAIL :], lambda b: b + 2 if b % 4 < 2 else b + 6)
    far, beside, own_tail, perm = lax.optimization_barrier((far, beside, own_tail, perm))

    def reordered(rows):
        return jnp.dot(rows, perm, preferred_element_type=jnp.float32).astype(jnp.bfloat16)

    far = reordered(far)
    far_beside = permuted(far, lambda z, c, yy, xx: (z, c, yy, xx + 1))
    far_tail = permuted(far[BLOCK - TAIL :], lambda z, c, yy, xx: (z, c, yy, xx + 2))

    own, beside, own_tail = reordered(own), reordered(beside), reordered(own_tail)
    rows_in = (own, beside, far, far_beside, own_tail, far_tail)
    return block_output(where, rows_in, perm, conv_bias, weights)


def solution(mesh):
    finer = Mesh(mesh.devices.reshape(SIZES), AXES)
    seqa, seqb = AXES[:2], AXES[2:]
    in_specs = (P(AXES, None), P(None, seqa, None), P(None, seqa, None), P(), P(None, None, seqa))
    return jax.shard_map(
        local, mesh=finer, in_specs=in_specs, out_specs=P(AXES, None), check_vma=False
    )
```

```python
import jax
import jax.numpy as jnp
from jax import lax
from jax.experimental import pallas as pl
from jax.experimental.pallas import tpu as pltpu
from jax.sharding import Mesh
from jax.sharding import PartitionSpec as P

D = 640
LAYERS = 3
BLOCK = 512
TAIL = 128
AXES = ("zl", "core", "y", "zh", "x")
SIZES = (8, 2, 4, 2, 4)
DEVICES = 512
Z_SLOTS = (-1, 0, 1, 2, 3, 4, -3, -2)


def index_of(z, core, y, x):
    z, y, x = z % 16, y % 4, x % 4
    return (((z % 8) * 2 + core) * 4 + y) * 8 + (z // 8) * 4 + x


def permuted(value, target):
    pairs = []
    for z in range(16):
        for core in range(2):
            for y in range(4):
                for x in range(4):
                    pairs.append((index_of(z, core, y, x), index_of(*target(z, core, y, x))))
    return lax.ppermute(value, AXES, pairs)


def shifted(value, target):
    pairs = [(b, target(b)) for b in range(DEVICES)]
    return lax.ppermute(value, AXES, [(a, b) for a, b in pairs if b < DEVICES])


def from_z(value, by):
    return permuted(value, lambda z, core, y, x: (z - by, core, y, x))


def normed(values):
    scale = lax.rsqrt(jnp.mean(values * values, axis=1, keepdims=True) + 1e-06)
    return (values * scale).astype(jnp.bfloat16)


def kernel(
    where, s_ref, a_ref, r_ref, b_ref, ts_ref, tr_ref, perm_ref, bias_ref,
    gathered, out_ref, taps, mix, x0, u1, u2, x1, u3, sems,
):
    x = where[0]

    def fetch(px, py, target, sem):
        for half in range(2):
            pltpu.make_async_copy(gathered.at[half * 16 + py * 4 + px], target(half * 320), sem).start()

    def fetch_mix(layer):
        fetch(layer, 3, lambda row: mix.at[layer, pl.ds(row, 320)], sems.at[3 + layer])

    def fetch_taps(layer):
        for px in range(4):
            rows, columns = (px // 2) * D, pl.ds((px % 2) * D, D)
            fetch(px, layer, lambda row: taps.at[layer, pl.ds(rows + row, 320), columns], sems.at[layer])

    for index in range(LAYERS):
        fetch_taps(index)
        fetch_mix(index)

    def ready(layer):
        pltpu.make_async_copy(taps.at[layer], taps.at[layer], sems.at[layer]).wait()
        pltpu.make_async_copy(mix.at[layer], mix.at[layer], sems.at[3 + layer]).wait()

    def bring(ref, slot, tail_slot):
        x0[slot] = ref[...]
        unit = normed(ref[...].astype(jnp.float32))
        u1[slot, TAIL:] = unit
        if tail_slot is not None:
            u1[tail_slot, :TAIL] = unit[BLOCK - TAIL :]

    def bring_tail(ref, slot):
        u1[slot, :TAIL] = normed(ref[...].astype(jnp.float32))

    a_slot = jnp.where(x == 0, 0, 2)
    t_slot = jnp.where(x < 2, 0, 2)
    bring(s_ref, 3, None)
    bring(r_ref, 1, None)
    bring(a_ref, a_slot, a_slot + 1)
    bring(b_ref, 2 - a_slot, 3 - a_slot)
    bring_tail(ts_ref, t_slot)
    bring_tail(tr_ref, 2 - t_slot)

    def layer(prev, now, held, index):
        both = jnp.concatenate([prev, now], axis=1)
        pre = jnp.dot(both, taps[index], preferred_element_type=jnp.float32)
        pre = pre + bias_ref[index : index + 1, :]
        hidden = (pre[:, :D] * jax.nn.sigmoid(pre[:, D:])).astype(jnp.bfloat16)
        return held + lax.dot_general(
            hidden, mix[index], (((1,), (1,)), ((), ())), preferred_element_type=jnp.float32
        )

    ready(0)

    def keep(slot, unit):
        return jnp.where(where[1 + slot] != 0, unit, jnp.zeros_like(unit))

    def two(ref, first, second, rows):
        return jnp.concatenate([ref[first, rows], ref[second, rows]], axis=0)

    def first_layer(pair):
        low, high = 2 * pair, 2 * pair + 1
        prev = two(u1, low, high, pl.ds(0, BLOCK))
        now = two(u1, low, high, pl.ds(TAIL, BLOCK))
        after = layer(prev, now, two(x0, low, high, pl.ds(0, BLOCK)).astype(jnp.float32), 0)
        unit = normed(after)
        u2[low] = keep(low, unit[:BLOCK])
        u2[high] = keep(high, unit[BLOCK:])
        x1[pair] = after[BLOCK:]

    pl.loop(0, 2)(first_layer)

    ready(1)
    after = layer(two(u2, 0, 2, slice(None)), two(u2, 1, 3, slice(None)), jnp.concatenate([x1[0], x1[1]], axis=0), 1)
    unit = normed(after)
    u3[0] = keep(1, unit[:BLOCK])
    u3[1] = unit[BLOCK:]
    x1[1] = after[BLOCK:]

    ready(2)
    after = layer(u3[0], u3[1], x1[1], 2).astype(jnp.bfloat16)
    out_ref[...] = lax.dot_general(
        after, perm_ref[...], (((1,), (1,)), ((), ())), preferred_element_type=jnp.float32
    ).astype(jnp.bfloat16)


def block_output(where, rows_in, perm, bias, weights):
    vmem = pl.BlockSpec(memory_space=pltpu.VMEM)
    hbm = pl.BlockSpec(memory_space=pl.ANY)
    return pl.pallas_call(
        kernel,
        out_shape=jax.ShapeDtypeStruct((BLOCK, D), jnp.bfloat16),
        in_specs=[pl.BlockSpec(memory_space=pltpu.SMEM)] + [vmem] * 8 + [hbm],
        out_specs=vmem,
        scratch_shapes=[
            pltpu.VMEM((3, 2 * D, 2 * D), jnp.bfloat16),
            pltpu.VMEM((3, D, D), jnp.bfloat16),
            pltpu.VMEM((4, BLOCK, D), jnp.bfloat16),
            pltpu.VMEM((4, TAIL + BLOCK, D), jnp.bfloat16),
            pltpu.VMEM((4, BLOCK, D), jnp.bfloat16),
            pltpu.VMEM((2, BLOCK, D), jnp.float32),
            pltpu.VMEM((2, BLOCK, D), jnp.bfloat16),
            pltpu.SemaphoreType.DMA((6,)),
        ],
        compiler_params=pltpu.CompilerParams(vmem_limit_bytes=56 * 1024 * 1024),
        cost_estimate=pl.CostEstimate(flops=15_000_000_000, bytes_accessed=16_000_000, transcendentals=3_000_000),
    )(where, *rows_in, perm, bias, weights)


def local(sequence_input, w_prev, w_now, conv_bias, w_mix):
    zl, core, y, zh, x = (lax.axis_index(a) for a in AXES)
    block = (((zl * 2 + core) * 4 + y) * 2 + zh) * 4 + x

    at = jnp.minimum(y, 2)
    tap_prev = lax.dynamic_slice(w_prev, (at, 0, (x % 2) * D), (1, 40, D))[0]
    tap_now = lax.dynamic_slice(w_now, (at, 0, (x % 2) * D), (1, 40, D))[0]
    mixing = lax.dynamic_slice(w_mix, (jnp.minimum(x, 2), 0, 0), (1, D, 40))[0].T
    piece = jnp.where(y == 3, mixing, jnp.where(x < 2, tap_prev, tap_now))

    own = sequence_input
    stepped = lax.ppermute(
        own, AXES, [(b, b + 8) for b in range(DEVICES) if b % 8 >= 4 and b + 8 < DEVICES]
    )
    above, below = from_z(piece, 1), from_z(piece, -1)
    three = jnp.concatenate([below, piece, above])
    far_above, far_below = from_z(three, 3), from_z(three[40:], -3)
    near = jnp.concatenate([three, far_above, far_below])

    k = jnp.arange(D)
    shard = (zl + jnp.asarray(Z_SLOTS, jnp.int32)[(k % 320) // 40]) % 8
    channel = (shard * 2 + k // 320) * 40 + k % 40
    perm = (k[:, None] == channel[None, :]).astype(jnp.bfloat16)
    where = jnp.stack([x, block >= 5, block >= 4, block >= 1, block >= 0]).astype(jnp.int32)
    beside = shifted(own, lambda b: b + 1 if b % 4 < 3 else b + 5)
    near, own, stepped, beside = lax.optimization_barrier((near, own, stepped, beside))

    weights = lax.all_gather(near, ("core", "y", "x"))
    far = permuted(
        jnp.where(zh == 1, stepped, own), lambda z, c, yy, xx: (z + 8, c, yy, xx)
    )
    own_tail = shifted(own[BLOCK - TAIL :], lambda b: b + 2 if b % 4 < 2 else b + 6)
    def reordered(rows):
        return jnp.dot(rows, perm, preferred_element_type=jnp.float32).astype(jnp.bfloat16)

    ready = reordered(own), reordered(beside)
    far, ready, own_tail, perm = lax.optimization_barrier((far, ready, own_tail, perm))

    far = reordered(far)
    far_beside = permuted(far, lambda z, c, yy, xx: (z, c, yy, xx + 1))
    far_tail = permuted(far[BLOCK - TAIL :], lambda z, c, yy, xx: (z, c, yy, xx + 2))

    rows_in = (*ready, far, far_beside, reordered(own_tail), far_tail)
    return block_output(where, rows_in, perm, conv_bias, weights)


def solution(mesh):
    finer = Mesh(mesh.devices.reshape(SIZES), AXES)
    seqa, seqb = AXES[:2], AXES[2:]
    in_specs = (P(AXES, None), P(None, seqa, None), P(None, seqa, None), P(), P(None, None, seqa))
    return jax.shard_map(
        local, mesh=finer, in_specs=in_specs, out_specs=P(AXES, None), check_vma=False
    )
```
